32 devices in a mesh: ma: 4 (over y, x), af: 8 (over z, core).
Axes of the slice: x: 2, y: 2, z: 4, core: 2. Of those that a mesh axis runs over, the one named last changes fastest.
Arguments:
- beams: bfloat16 [4, 8, 4, 512, 2048], P(None, 'af', 'ma'), may hold values from -2 to 2
- spectrum: float32 [32, 3, 1024], P('af'), may hold values from 0.3 to 3
- partners: int32 [32, 3], P('af'), may hold values from 0 to 31, as said below
Outputs:
- covariance: bfloat16 [4, 32, 3, 2, 512, 512], P('ma', 'af')
The draws below stay inside these ranges and needn't reach their ends.
Inputs may be any that keep to these rules, and one draw needn't show every extreme that they name: partners[c, k] lies in the band of c (channels 64 * (c // 64) up to the band's end or the last channel) and at most 2 channels from c; the distance 2 occurs.
All inputs are finite; a program needn't handle non-finite values.
Results may differ from the reference program's by a relative error of at most 0.0044.
Values may be sent and summed in bfloat16 or wider, within the bound.
A program may use at most 192 MiB of HBM per device.

```python
import math
import jax
import jax.numpy as jnp
from jax import lax

NB = 512
NL = 1024
FL = 4
K = 3
REACH = 2
BAND = 64
M = 4
FH = 8
F = 32


def draw_partners(key, part):
    key = jax.random.fold_in(key, 7)
    channel = jnp.arange(F, dtype=jnp.int32)[:, None]
    offsets = jax.random.randint(key, (F, K), -REACH, REACH + 1, dtype=jnp.int32)
    lower = channel // BAND * BAND
    upper = jnp.minimum(lower + BAND, F) - 1
    chosen = jnp.clip(channel + offsets, lower, upper)
    chosen = chosen.at[0, K - 1].set(REACH)
    chosen = chosen.at[0, 0].set(0)
    chosen = chosen.at[F - 1, 0].set(F - 1)
    return chosen


def block_scale(key, shape, split, low, top_value):
    def one(dim, parts):
        draws = jax.random.uniform(jax.random.fold_in(jax.random.fold_in(key, 6), dim), (parts,), jnp.float32, low / len(split), top_value / len(split))
        return jnp.repeat(jnp.exp(draws), shape[dim] // parts).reshape((-1,) + (1,) * (len(shape) - dim - 1))

    gain = one(*split[0])
    for cut in split[1:]:
        gain = gain * one(*cut)
    return gain


def bell_draw(rng, dims, width, limit, split=(), kind=jnp.bfloat16):
    result = width * jax.random.normal(rng, dims, jnp.float32)
    if split:
        result = result * block_scale(rng, dims, split, -0.22, 0.18)
    return jnp.clip(result, -limit, limit).astype(kind)


def setup_inputs(seed: int = 0) -> dict:
    seeds = jax.random.split(jax.random.key(seed), 4)
    beams = bell_draw(seeds[0], (M, FH, FL, NB, 2 * NL), ((2 * NL) ** -0.25), 2.0, ((1, 8), (2, 4)))
    spectrum = jnp.clip(jnp.exp(math.log(3.0) - 2.3025851 * jax.random.uniform(seeds[1], (F, K, NL), jnp.float32) ** block_scale(seeds[1], (F, K, NL), ((0, 8),), -0.2, 0.2)), 0.3, 3.0)
    partners = draw_partners(jax.random.fold_in(seeds[3], 71), 0)
    return dict(beams=beams, spectrum=spectrum, partners=partners)


def sandwich(own, right, weights):
    half = own.shape[-1] // 2
    real_part = own[:, :half].astype(jnp.float32) * weights
    imag_part = own[:, half:].astype(jnp.float32) * weights
    upper = jnp.concatenate([real_part, imag_part], axis=1)
    lower = jnp.concatenate([imag_part, -real_part], axis=1)
    left = jnp.concatenate([upper, lower], axis=0).astype(jnp.bfloat16)
    product = jnp.dot(left, right.T, preferred_element_type=jnp.float32)
    return product.astype(jnp.bfloat16).reshape(2, own.shape[0], own.shape[0])


def reference(beams, spectrum, partners):
    flat = beams.reshape(M, F, NB, 2 * NL)
    results = []
    for mval in range(M):
        blocks = flat[mval]

        def one_channel(channel):
            own = lax.dynamic_index_in_dim(blocks, channel, 0, keepdims=False)
            weights = lax.dynamic_index_in_dim(spectrum, channel, 0, keepdims=False)
            targets = lax.dynamic_index_in_dim(partners, channel, 0, keepdims=False)
            outs = []
            for slot in range(K):
                right = lax.dynamic_index_in_dim(blocks, targets[slot].astype(jnp.int32), 0, keepdims=False)
                outs.append(sandwich(own, right, weights[slot]))
            return jnp.stack(outs, axis=0)

        results.append(lax.map(one_channel, jnp.arange(F, dtype=jnp.int32)))
    return jnp.stack(results, axis=0)
```

```python
import functools

import jax
import jax.numpy as jnp
from jax import lax
from jax.experimental import pallas as pl
from jax.experimental.pallas import tpu as pltpu
from jax.sharding import PartitionSpec as P

MESH = pl.DeviceIdType.MESH
REACH = 2
LANES = 128
AHEAD = 3
STAGES = 4


def flip(me, by, count):
    bit = 1
    peer = me
    while bit < count:
        if by & bit:
            peer = peer + bit * (1 - 2 * ((me // bit) % 2))
        bit *= 2
    return peer


def kernel(n_ma, n_af, chunks, partners, beams, spectrum, out, *scratch):
    ext = scratch[:chunks]
    acc, stage, a_send, a_recv, h_send, h_recv, own_sem, out_sem = scratch[chunks:]
    ma = lax.axis_index("ma")
    af = lax.axis_index("af")
    chans = n_ma
    rows = beams.shape[3]
    half = beams.shape[4] // 2
    slots = spectrum.shape[1]
    has_below = af > 0
    has_above = af < n_af - 1

    def remote(chunk, d, part):
        return pltpu.make_async_remote_copy(
            src_ref=beams.at[flip(ma, d, n_ma), 0, 0, :, pl.ds(part * half + chunk * LANES, LANES)],
            dst_ref=ext[chunk].at[REACH + ma, :, pl.ds(part * LANES, LANES)],
            send_sem=a_send.at[chunk, d - 1, part],
            recv_sem=a_recv.at[chunk, d - 1, part],
            device_id=(flip(ma, d, n_ma), af),
            device_id_type=MESH,
        )

    def arriving(chunk, d, part):
        return pltpu.make_async_remote_copy(
            src_ref=beams.at[flip(ma, d, n_ma), 0, 0, :, pl.ds(part * half + chunk * LANES, LANES)],
            dst_ref=ext[chunk].at[REACH + flip(ma, d, n_ma), :, pl.ds(part * LANES, LANES)],
            send_sem=a_send.at[chunk, d - 1, part],
            recv_sem=a_recv.at[chunk, d - 1, part],
            device_id=(flip(ma, d, n_ma), af),
            device_id_type=MESH,
        )

    def local(chunk, part):
        return pltpu.make_async_copy(
            beams.at[ma, 0, 0, :, pl.ds(part * half + chunk * LANES, LANES)],
            ext[chunk].at[REACH + ma, :, pl.ds(part * LANES, LANES)],
            own_sem.at[chunk, part],
        )

    def down(chunk):
        return pltpu.make_async_remote_copy(
            src_ref=ext[chunk].at[pl.ds(REACH, REACH)],
            dst_ref=ext[chunk].at[pl.ds(REACH + chans, REACH)],
            send_sem=h_send.at[chunk, 0],
            recv_sem=h_recv.at[chunk, 0],
            device_id=(ma, af - 1),
            device_id_type=MESH,
        )

    def up(chunk):
        return pltpu.make_async_remote_copy(
            src_ref=ext[chunk].at[pl.ds(chans, REACH)],
            dst_ref=ext[chunk].at[pl.ds(0, REACH)],
            send_sem=h_send.at[chunk, 1],
            recv_sem=h_recv.at[chunk, 1],
            device_id=(ma, af + 1),
            device_id_type=MESH,
        )

    parts = [(d, part) for d in range(1, n_ma) for part in range(2)]

    def launch(chunk):
        for d, part in parts:
            remote(chunk, d, part).start()
        for part in range(2):
            local(chunk, part).start()

    barrier = pltpu.get_barrier_semaphore()
    for d in range(1, n_ma):
        pl.semaphore_signal(barrier, inc=1, device_id=(flip(ma, d, n_ma), af), device_id_type=MESH)

    @pl.when(has_below)
    def _():
        pl.semaphore_signal(barrier, inc=1, device_id=(ma, af - 1), device_id_type=MESH)

    @pl.when(has_above)
    def _():
        pl.semaphore_signal(barrier, inc=1, device_id=(ma, af + 1), device_id_type=MESH)

    peers = n_ma - 1 + has_below.astype(jnp.int32) + has_above.astype(jnp.int32)
    pl.semaphore_wait(barrier, peers)

    for chunk in range(min(AHEAD, chunks)):
        launch(chunk)

    def forward(chunk):
        for d, part in parts:
            arriving(chunk, d, part).wait_recv()
        for part in range(2):
            local(chunk, part).wait()

        @pl.when(has_below)
        def _():
            down(chunk).start()

        @pl.when(has_above)
        def _():
            up(chunk).start()

    def halo_wait(chunk):
        @pl.when(has_above)
        def _():
            down(chunk).wait_recv()

        @pl.when(has_below)
        def _():
            up(chunk).wait_recv()

    def to_hbm(item):
        return pltpu.make_async_copy(
            stage.at[item % STAGES], out.at[0, item // slots, item % slots], out_sem.at[item % STAGES]
        )

    def compute(chunk):
        data = ext[chunk]
        first, last = chunk == 0, chunk == chunks - 1

        @pl.loop(0, chans * slots)
        def _(item):
            channel = item // slots
            slot = item % slots
            where = jnp.clip(partners[channel, slot] - af * chans + REACH, 0, chans + 2 * REACH - 1)
            right = data[where]
            own = data[REACH + channel]
            every = spectrum[channel, :, chunk * LANES : (chunk + 1) * LANES]
            weights = every[:1]
            for other in range(1, slots):
                weights = jnp.where(slot == other, every[other : other + 1], weights)
            real = own[:, :LANES].astype(jnp.float32) * weights
            imag = own[:, LANES:].astype(jnp.float32) * weights
            upper = jnp.concatenate([real, imag], axis=1).astype(jnp.bfloat16)
            lower = jnp.concatenate([imag, -real], axis=1).astype(jnp.bfloat16)
            if last:
                @pl.when(item >= STAGES)
                def _():
                    to_hbm(item - STAGES).wait()

            for index, left in enumerate((upper, lower)):
                product = lax.dot_general(
                    left, right, (((1,), (1,)), ((), ())), preferred_element_type=jnp.float32
                )
                if not first:
                    product = product + acc[item, index]
                if last:
                    stage[item % STAGES, index] = product.astype(jnp.bfloat16)
                else:
                    acc[item, index] = product
            if last:
                to_hbm(item).start()

    for chunk in range(chunks):
        forward(chunk)
        if chunk + AHEAD < chunks:
            launch(chunk + AHEAD)
        if chunk > 0:
            halo_wait(chunk - 1)
            compute(chunk - 1)
    halo_wait(chunks - 1)
    compute(chunks - 1)

    for item in range(chans * slots - STAGES, chans * slots):
        to_hbm(item).wait()
    for chunk in range(chunks):
        for d, part in parts:
            remote(chunk, d, part).wait_send()

        @pl.when(has_below)
        def _():
            down(chunk).wait_send()

        @pl.when(has_above)
        def _():
            up(chunk).wait_send()


def solution(mesh):
    n_ma, n_af = mesh.shape["ma"], mesh.shape["af"]

    def body(beams, spectrum, partners):
        rows, width = beams.shape[3], beams.shape[4]
        chans, slots = partners.shape
        chunks = width // 2 // LANES
        chunk_shape = (chans + 2 * REACH, rows, 2 * LANES)
        flops = 2 * chans * slots * 2 * rows * rows * width
        return pl.pallas_call(
            functools.partial(kernel, n_ma, n_af, chunks),
            out_shape=jax.ShapeDtypeStruct((1, chans, slots, 2, rows, rows), jnp.bfloat16),
            in_specs=[
                pl.BlockSpec(memory_space=pltpu.SMEM),
                pl.BlockSpec(memory_space=pl.ANY),
                pl.BlockSpec(memory_space=pltpu.VMEM),
            ],
            out_specs=pl.BlockSpec(memory_space=pl.ANY),
            scratch_shapes=[pltpu.VMEM(chunk_shape, jnp.bfloat16) for _ in range(chunks)]
            + [
                pltpu.VMEM((chans * slots, 2, rows, rows), jnp.float32),
                pltpu.VMEM((STAGES, 2, rows, rows), jnp.bfloat16),
                pltpu.SemaphoreType.DMA((chunks, n_ma - 1, 2)),
                pltpu.SemaphoreType.DMA((chunks, n_ma - 1, 2)),
                pltpu.SemaphoreType.DMA((chunks, 2)),
                pltpu.SemaphoreType.DMA((chunks, 2)),
                pltpu.SemaphoreType.DMA((chunks, 2)),
                pltpu.SemaphoreType.DMA((STAGES,)),
            ],
            compiler_params=pltpu.CompilerParams(
                collective_id=0, has_side_effects=True, vmem_limit_bytes=58 * 2**20
            ),
            cost_estimate=pl.CostEstimate(flops=flops, bytes_accessed=28 * 2**20, transcendentals=0),
        )(partners, beams, spectrum)

    in_specs = (P(None, "af", "ma", None, None), P("af", None, None), P("af", None))
    out_specs = P("ma", "af", None, None, None, None)
    return jax.shard_map(body, mesh=mesh, in_specs=in_specs, out_specs=out_specs, check_vma=False)
```
